128 devices in a mesh: item: 32 (over y, x, core), user: 4 (over z).
Axes of the slice: x: 4, y: 4, z: 4, core: 2. Of those that a mesh axis runs over, the one named last changes fastest.
Arguments:
- tiles: float32 [768, 32, 128, 128], P('user', 'item'), may hold values from -6 to 6
- tile_user: int32 [768, 32], P('user', 'item'), may hold values from 0 to 31
- tile_item: int32 [768, 32], P('user', 'item'), may hold values from 0 to 127
- row_lengths: int32 [768, 32, 128], P('user', 'item'), may hold values from 1 to 128
- start_panel: float32 [524288, 64], P('item'), may hold values from -6 to 6
Outputs:
- panel: float32 [524288, 64], P('item')
The draws below stay inside these ranges and needn't reach their ends.
All inputs are finite; a program needn't handle non-finite values.
Results may differ from the reference program's by a relative error of at most 0.0003.
Values sent between devices are 32-bit elements; how exact they have to be, the bound alone decides.
No kernel may reach another device: no remote copies, remote signals or barrier semaphores. Data moves between devices by JAX's collectives and lax.ppermute only.
A program may use at most 128 MiB of HBM per device.

```python
import jax
import jax.numpy as jnp
from jax import lax

K = 64
TB = 128
ITERS = 2
ITEM_DEV = 16384
USER_DEV = 4096
NT = 192
ITEMS = 524288
USERS = 16384
SLOTS = 768
GROUPS = 32
N_ITEM = 32
N_USER = 4


def touch_ends(array, key, smallest, top_value):
    spot = [jax.random.randint(jax.random.fold_in(key, axis), (), 0, length) for axis, length in enumerate(array.shape)]
    widest = array.shape.index(max(array.shape))
    beside = spot[:widest] + [(spot[widest] + 1) % array.shape[widest]] + spot[widest + 1:]
    return array.at[tuple(spot)].set(smallest).at[tuple(beside)].set(top_value)


def levels(key, extent, shards, smallest, largest):
    loudness = 1.0
    for axis_at, blocks in shards:
        steps = jax.random.uniform(jax.random.fold_in(jax.random.fold_in(key, 6), axis_at), (blocks,), jnp.float32, smallest / len(shards), largest / len(shards))
        loudness = loudness * jnp.repeat(jnp.exp(steps), extent[axis_at] // blocks).reshape((-1,) + (1,) * (len(extent) - 1 - axis_at))
    return loudness


def noise(own_key, dims, spread, most, pieces=(), held_as=jnp.bfloat16):
    values = spread * jax.random.normal(own_key, dims, jnp.float32)
    if pieces:
        values = values * levels(own_key, dims, pieces, -0.22, 0.18)
    return jnp.clip(values, -most, most).astype(held_as)


def setup_inputs(seed: int = 0) -> dict:
    seeds = jax.random.split(jax.random.key(seed), 6)
    return {
        "tiles": noise(seeds[0], (SLOTS, GROUPS, TB, TB), 1.0, 6.0, ((0, 4), (1, 32)), jnp.float32),
        "tile_user": touch_ends(jax.random.randint(seeds[1], (SLOTS, GROUPS), 0, USER_DEV // TB), jax.random.fold_in(seeds[1], 1), 0, (USER_DEV // TB) - 1).astype(jnp.int32),
        "tile_item": touch_ends(jax.random.randint(seeds[2], (SLOTS, GROUPS), 0, ITEM_DEV // TB), jax.random.fold_in(seeds[2], 1), 0, (ITEM_DEV // TB) - 1).astype(jnp.int32),
        "row_lengths": touch_ends(jax.random.randint(seeds[3], (SLOTS, GROUPS, TB), 1, TB + 1), jax.random.fold_in(seeds[3], 1), 1, TB).astype(jnp.int32),
        "start_panel": noise(seeds[4], (ITEMS, K), 1.0, 6.0, ((0, 32),), jnp.float32),
    }


def masked_group(tiles_u, lengths_u):
    columns = lax.broadcasted_iota(jnp.int32, tiles_u.shape, 3)
    return jnp.where(columns < lengths_u[..., None], tiles_u, jnp.float32(0.0))

def global_items(item_u):
    offsets = (jnp.arange(N_ITEM, dtype=jnp.int32) * (ITEM_DEV // TB)).astype(jnp.int32)
    return (item_u + offsets[None, :]).astype(jnp.int32)

def apply_x(tiles, tile_user, tile_item, row_lengths, panel):
    blocks = panel.reshape(ITEMS // TB, TB, K)

    def one(args):
        tiles_u, lengths_u, user_u, item_u = args
        masked = masked_group(tiles_u, lengths_u)
        picked = blocks[global_items(item_u)]
        product = jnp.einsum('nirc,nick->nirk', masked, picked, precision=lax.Precision.HIGHEST)
        return jax.ops.segment_sum(product.reshape(-1, TB, K), user_u.reshape(-1), num_segments=USER_DEV // TB)
    result = lax.map(one, (tiles.reshape(N_USER, NT, N_ITEM, TB, TB), row_lengths.reshape(N_USER, NT, N_ITEM, TB), tile_user.reshape(N_USER, NT, N_ITEM), tile_item.reshape(N_USER, NT, N_ITEM)))
    return result.reshape(USERS, K)

def apply_xt(tiles, tile_user, tile_item, row_lengths, users):
    user_blocks = users.reshape(N_USER, USER_DEV // TB, TB, K)

    def one(args):
        tiles_u, lengths_u, user_u, item_u, blocks_u = args
        masked = masked_group(tiles_u, lengths_u)
        picked = blocks_u[user_u]
        product = jnp.einsum('nirc,nirk->nick', masked, picked, precision=lax.Precision.HIGHEST)
        return jax.ops.segment_sum(product.reshape(-1, TB, K), global_items(item_u).reshape(-1), num_segments=ITEMS // TB)
    result = lax.map(one, (tiles.reshape(N_USER, NT, N_ITEM, TB, TB), row_lengths.reshape(N_USER, NT, N_ITEM, TB), tile_user.reshape(N_USER, NT, N_ITEM), tile_item.reshape(N_USER, NT, N_ITEM), user_blocks))
    return jnp.sum(result, axis=0).reshape(ITEMS, K)

def reference(tiles, tile_user, tile_item, row_lengths, start_panel):
    users = apply_x(tiles, tile_user, tile_item, row_lengths, start_panel)
    panel = start_panel
    for step in range(ITERS):
        cross = apply_xt(tiles, tile_user, tile_item, row_lengths, users)
        gram = jnp.dot(cross.T.astype(jnp.float32), cross.astype(jnp.float32), precision=lax.Precision.HIGHEST, preferred_element_type=jnp.float32) / ITEMS
        lower = jnp.linalg.cholesky(gram)
        panel = lax.linalg.triangular_solve(lower, cross, left_side=False, lower=True, transpose_a=True)
        if step + 1 < ITERS:
            users = apply_x(tiles, tile_user, tile_item, row_lengths, panel)
    return panel
```

```python
import functools

import jax
import jax.numpy as jnp
from jax import lax
from jax.experimental import pallas as pl
from jax.experimental.pallas import tpu as pltpu
from jax.sharding import PartitionSpec as P

ITERS = 2
TB = 128
K = 64
NT = 192
IB = 128
UB = 32
QB = 32
HB = 16
ITEMS = 524288
GROUP = 8
VMEM = pl.BlockSpec(memory_space=pltpu.VMEM)
SMEM = pl.BlockSpec(memory_space=pltpu.SMEM)
ANY = pl.BlockSpec(memory_space=pl.ANY)
LIMIT = 48 * 1024 * 1024
F32, BF16 = jnp.float32, jnp.bfloat16


def split2(x):
    hi = x.astype(BF16)
    lo = (x - hi.astype(F32)).astype(BF16)
    return hi, lo


def split3(x):
    hi = x.astype(BF16)
    rest = x - hi.astype(F32)
    mid = rest.astype(BF16)
    lo = (rest - mid.astype(F32)).astype(BF16)
    return hi, mid, lo


def times_nt(block, stacked):
    left = jnp.concatenate(split2(block), axis=0)
    full = lax.dot_general(left, stacked, (((1,), (1,)), ((), ())), preferred_element_type=F32)
    half = full[:K] + full[K:]
    return half[:, :TB] + half[:, TB:]


def times_nn(block, stacked):
    hi, lo = split2(block)
    left = jnp.concatenate(
        [jnp.concatenate([hi, hi], axis=1), jnp.concatenate([lo, lo], axis=1)], axis=0
    )
    full = lax.dot_general(left, stacked, (((1,), (0,)), ((), ())), preferred_element_type=F32)
    return full[:K] + full[K:]


def first_kernel(upos, item, tiles, lengths, panel, users, stacked):
    step = pl.program_id(0)

    @pl.when(step == 0)
    def _():
        users[...] = jnp.zeros_like(users)

    columns = lax.broadcasted_iota(jnp.int32, (TB, TB), 1)
    parts = []
    for t in range(GROUP):
        n = step * GROUP + t
        masked = jnp.where(columns < lengths[0, :, t : t + 1], tiles[t], 0.0)
        both = jnp.concatenate(split2(masked), axis=0)
        stacked[t] = both
        block = panel[:, pl.ds(pl.multiple_of(item[n] * TB, TB), TB)]
        parts.append((upos[n], times_nt(block, both)))
    for spot, value in parts:
        users[spot] += value


def first_product(upos, item, tiles, lengths, panel_t):
    steps = NT // GROUP
    return pl.pallas_call(
        first_kernel,
        out_shape=(
            jax.ShapeDtypeStruct((UB, K, TB), F32),
            jax.ShapeDtypeStruct((NT, 2 * TB, TB), BF16),
        ),
        grid_spec=pltpu.PrefetchScalarGridSpec(
            num_scalar_prefetch=2,
            grid=(steps,),
            in_specs=[
                pl.BlockSpec((GROUP, TB, TB), lambda s, *_: (s, 0, 0)),
                pl.BlockSpec((1, TB, GROUP), lambda s, *_: (s, 0, 0)),
                pl.BlockSpec((K, IB * TB), lambda s, *_: (0, 0)),
            ],
            out_specs=[
                pl.BlockSpec((UB, K, TB), lambda s, *_: (0, 0, 0)),
                pl.BlockSpec((GROUP, 2 * TB, TB), lambda s, *_: (s, 0, 0)),
            ],
        ),
        compiler_params=pltpu.CompilerParams(vmem_limit_bytes=LIMIT),
    )(upos, item, tiles, lengths, panel_t)


def load_tiles(order, bounds, which, stacked, held, sems):
    start, end = bounds[which], bounds[which + 1]

    def begin(j, carry):
        pltpu.make_async_copy(stacked.at[order[j]], held.at[j - start], sems.at[j - start]).start()
        return carry

    lax.fori_loop(start, end, begin, 0)
    return start, end


def each_tile(start, end, stacked, held, sems, unroll, use):
    def group(g, carry):
        parts = []
        for t in range(unroll):
            j = start + g * unroll + t
            valid = j < end
            at = jnp.minimum(j, end - 1)

            @pl.when(valid)
            def _():
                pltpu.make_async_copy(stacked.at[0], held.at[at - start], sems.at[at - start]).wait()

        for t in range(unroll):
            j = start + g * unroll + t
            at = jnp.minimum(j, end - 1)
            ref, spot, value = use(at, held.at[at - start])
            parts.append((ref, spot, jnp.where(j < end, value, 0.0)))
        for ref, spot, value in parts:
            ref[spot] += value
        return carry

    lax.fori_loop(0, (end - start + unroll - 1) >> (unroll.bit_length() - 1), group, 0)


def back_kernel(which, blocks, order, upos, ipos, bounds, users, stacked, *rest):
    outs = rest[: blocks // HB]
    held, sems, total = rest[blocks // HB :]
    start, end = load_tiles(order, bounds, which, stacked, held, sems)
    total[...] = jnp.zeros_like(total)

    def use(at, tile):
        return total, ipos[at], times_nn(users[upos[at]], tile[...])

    each_tile(start, end, stacked, held, sems, 4, use)
    for number, out in enumerate(outs):
        out[...] = total[number * HB : (number + 1) * HB]


def back_product(which, blocks, lists, users, stacked):
    return pl.pallas_call(
        functools.partial(back_kernel, which, blocks),
        out_shape=[jax.ShapeDtypeStruct((HB, K, TB), F32)] * (blocks // HB),
        in_specs=[SMEM] * 4 + [VMEM, ANY],
        out_specs=[VMEM] * (blocks // HB),
        scratch_shapes=[
            pltpu.VMEM((NT, 2 * TB, TB), BF16),
            pltpu.SemaphoreType.DMA((NT,)),
            pltpu.VMEM((blocks, K, TB), F32),
        ],
        compiler_params=pltpu.CompilerParams(vmem_limit_bytes=LIMIT),
    )(*lists, users, stacked)


def forth_kernel(which, pieces, more, order, upos, ipos, bounds, stacked, *rest):
    ins = rest[:pieces]
    rest = rest[pieces:]
    if more:
        before, rest = rest[0], rest[1:]
    out, held, sems, panel = rest
    start, end = load_tiles(order, bounds, which, stacked, held, sems)
    out[...] = before[...] if more else jnp.zeros_like(out)
    for number, piece in enumerate(ins):
        panel[number * HB : (number + 1) * HB] = piece[...]

    def use(at, tile):
        return out, upos[at], times_nt(panel[ipos[at]], tile[...])

    each_tile(start, end, stacked, held, sems, 4, use)


def forth_product(which, lists, stacked, pieces, before=None):
    more = before is not None
    args = list(pieces) + ([before] if more else [])
    return pl.pallas_call(
        functools.partial(forth_kernel, which, len(pieces), more),
        out_shape=jax.ShapeDtypeStruct((UB, K, TB), F32),
        in_specs=[SMEM] * 4 + [ANY] + [VMEM] * len(args),
        out_specs=VMEM,
        scratch_shapes=[
            pltpu.VMEM((NT, 2 * TB, TB), BF16),
            pltpu.SemaphoreType.DMA((NT,)),
            pltpu.VMEM((len(pieces) * HB, K, TB), F32),
        ],
        compiler_params=pltpu.CompilerParams(vmem_limit_bytes=LIMIT),
    )(*lists, stacked, *args)


def gram_kernel(first, second, out):
    total = jnp.zeros((3 * K, 3 * K), F32)
    for ref in (first, second):
        for b in range(0, HB, 2):
            three = jnp.concatenate(split3(jnp.concatenate([ref[b], ref[b + 1]], axis=1)), axis=0)
            total += lax.dot_general(
                three, three, (((1,), (1,)), ((), ())), preferred_element_type=F32
            )
    rows = (total[2 * K :] + total[K : 2 * K]) + total[:K]
    out[...] = (rows[:, 2 * K :] + rows[:, K : 2 * K]) + rows[:, :K]


def gram_product(first, second):
    return pl.pallas_call(
        gram_kernel,
        out_shape=jax.ShapeDtypeStruct((K, K), F32),
        in_specs=[VMEM] * 2,
        out_specs=VMEM,
        compiler_params=pltpu.CompilerParams(vmem_limit_bytes=LIMIT),
    )(first, second)


def inverse_kernel(gram, out):
    rows = lax.broadcasted_iota(jnp.int32, (K, 2 * K), 0)
    lanes = lax.broadcasted_iota(jnp.int32, (K, 2 * K), 1)
    unit = (lanes == rows + K).astype(F32)
    left = gram[...] * F32(1.0 / ITEMS)
    work = jnp.concatenate([left, jnp.zeros((K, K), F32)], axis=1) + unit
    for k in range(K):
        pivot = work[k : k + 1, k : k + 1]
        scaled = work[k : k + 1, :] * lax.rsqrt(pivot)
        column = work[:, k : k + 1] * lax.rsqrt(pivot)
        lower = work - column * scaled
        work = jnp.where(rows > k, lower, jnp.where(rows == k, scaled, work))
    out[...] = work[:, K:]


def inverse_lower(gram):
    return pl.pallas_call(
        inverse_kernel,
        out_shape=jax.ShapeDtypeStruct((K, K), F32),
        in_specs=[VMEM],
        out_specs=VMEM,
    )(gram)


def scale_kernel(inverse, users, out):
    for b in range(UB):
        out[b] = jnp.dot(
            inverse[...], users[b], precision=lax.Precision.HIGHEST, preferred_element_type=F32
        )


def scale_users(inverse, users):
    return pl.pallas_call(
        scale_kernel,
        out_shape=jax.ShapeDtypeStruct((UB, K, TB), F32),
        in_specs=[VMEM] * 2,
        out_specs=VMEM,
        compiler_params=pltpu.CompilerParams(vmem_limit_bytes=LIMIT),
    )(inverse, users)


def final_kernel(base, inverse, *refs):
    pieces, out = refs[:-1], refs[-1]
    for number, piece in enumerate(pieces):
        spot = base[number >> 1] + (number & 1) * (HB * TB)
        for b in range(HB):
            at = pl.multiple_of(spot + b * TB, TB)
            out[:, pl.ds(at, TB)] = jnp.dot(
                inverse[...], piece[b], precision=lax.Precision.HIGHEST, preferred_element_type=F32
            )


def final_product(base, inverse, pieces):
    return pl.pallas_call(
        final_kernel,
        out_shape=jax.ShapeDtypeStruct((K, IB * TB), F32),
        in_specs=[SMEM] + [VMEM] * (1 + len(pieces)),
        out_specs=VMEM,
        compiler_params=pltpu.CompilerParams(vmem_limit_bytes=LIMIT),
    )(base, inverse, *pieces)


def user_move(value, by):
    return lax.ppermute(value, "user", [(s, (s + by) % 4) for s in range(4)])


def item_move(value, dy=0, dx=0, dc=0):
    pairs = []
    for y in range(4):
        for x in range(4):
            for c in range(2):
                to = (((y + dy) % 4) * 4 + (x + dx) % 4) * 2 + (c + dc) % 2
                pairs.append(((y * 4 + x) * 2 + c, to))
    return lax.ppermute(value, "item", pairs)


def sum_over_item(part):
    mine = part[:16] + item_move(part[16:], dc=1)
    near, right, far, left = mine[:4], mine[4:8], mine[8:12], mine[12:]
    mine = near + item_move(right, dx=1) + item_move(left, dx=-1) + item_move(far, dx=2)
    one, two, three = item_move(mine, dy=1), item_move(mine, dy=2), item_move(mine, dy=-1)
    mine = (mine + jnp.roll(two, 2, 0)) + (jnp.roll(one, -1, 0) + jnp.roll(three, 1, 0))
    left, far, right = item_move(mine, dx=1), item_move(mine, dx=2), item_move(mine, dx=-1)
    mine = jnp.concatenate([mine, right, far, left], axis=0)
    return jnp.concatenate([mine, item_move(mine, dc=1)], axis=0)


def sum_all(value):
    value = value + item_move(value, dc=1)
    value = (value + item_move(value, dx=2)) + (item_move(value, dx=1) + item_move(value, dx=-1))
    value = (value + item_move(value, dy=2)) + (item_move(value, dy=1) + item_move(value, dy=-1))
    return (value + user_move(value, 2)) + (user_move(value, 1) + user_move(value, -1))


def cross_pieces(users, lists, stacked):
    far_a, far_b = back_product(0, QB, lists, users, stacked)
    got_a, got_b = user_move(far_a, 1), user_move(far_b, -1)
    up_a, up_b, down_a, down_b = back_product(1, 2 * QB, lists, users, stacked)
    direct_b, direct_a = user_move(up_b, 1), user_move(down_a, -1)
    own_a, own_b = back_product(2, QB, lists, users, stacked)
    sum_a, sum_b = user_move(up_a + got_a, 1), user_move(down_b + got_b, -1)
    own_a, own_b = own_a + direct_a + sum_a, own_b + direct_b + sum_b
    below_a, above_b = user_move(own_a, 1), user_move(own_b, -1)
    below_b, above_a = user_move(own_b, 1), user_move(own_a, -1)
    far_a, far_b = user_move(below_a, 1), user_move(above_b, -1)
    return (own_a, own_b), (above_a, above_b, below_a, below_b), (far_a, far_b)


def body(tiles, tile_user, tile_item, row_lengths, start_panel):
    tiles = tiles.reshape(NT, TB, TB)
    user_block = tile_user.reshape(NT)
    item_block = tile_item.reshape(NT)
    lengths = row_lengths.reshape(NT // GROUP, GROUP, TB).transpose(0, 2, 1)
    spot = lax.axis_index("item")
    z = lax.axis_index("user")
    core, x, y = spot % 2, (spot // 2) % 4, spot // 8
    upos = ((user_block // 16) ^ core) * 16 + (((user_block // 4) % 4 - x) % 4) * 4 + (user_block % 4 - y) % 4
    quarter = (item_block // QB - z) % 4
    kind = jnp.where(quarter == 2, 0, jnp.where(quarter == 0, 2, 1))
    ipos = item_block % QB + jnp.where(quarter == 3, QB, 0)
    number = jnp.arange(NT, dtype=jnp.int32)
    key = kind * NT + number
    rank = jnp.sum((key[None, :] < key[:, None]).astype(jnp.int32), axis=1)
    place = rank[None, :] == number[:, None]
    order = jnp.sum(jnp.where(place, number[None, :], 0), axis=1)
    upos_sorted = jnp.sum(jnp.where(place, upos[None, :], 0), axis=1)
    ipos_sorted = jnp.sum(jnp.where(place, ipos[None, :], 0), axis=1)
    bounds = jnp.sum((kind[None, :] < jnp.arange(4, dtype=jnp.int32)[:, None]).astype(jnp.int32), axis=1)
    lists = (order, upos_sorted, ipos_sorted, bounds)

    part, stacked = first_product(upos, item_block, tiles, lengths, start_panel.T)
    users = sum_over_item(part)
    own, near, far = cross_pieces(users, lists, stacked)
    inverse = inverse_lower(sum_all(gram_product(*own)))
    part = forth_product(2, lists, stacked, own)
    part = forth_product(1, lists, stacked, near, part)
    part = forth_product(0, lists, stacked, far, part)
    users = scale_users(inverse, sum_over_item(part))
    own, near, far = cross_pieces(users, lists, stacked)
    inverse = inverse_lower(sum_all(gram_product(*own)))
    base = ((z + jnp.array([0, 1, 3, 2], jnp.int32)) % 4) * (QB * TB)
    return final_product(base, inverse, own + near + far).T


def solution(mesh):
    placed = (
        P("user", "item", None, None),
        P("user", "item"),
        P("user", "item"),
        P("user", "item", None),
        P("item", None),
    )
    return jax.shard_map(
        body, mesh=mesh, in_specs=placed, out_specs=P("item", None), check_vma=False
    )
```

```python
import functools

import jax
import jax.numpy as jnp
from jax import lax
from jax.experimental import pallas as pl
from jax.experimental.pallas import tpu as pltpu
from jax.sharding import PartitionSpec as P

ITERS = 2
TB = 128
K = 64
NT = 192
IB = 128
UB = 32
QB = 32
HB = 16
ITEMS = 524288
GROUP = 48
RUN = 16
VMEM = pl.BlockSpec(memory_space=pltpu.VMEM)
SMEM = pl.BlockSpec(memory_space=pltpu.SMEM)
ANY = pl.BlockSpec(memory_space=pl.ANY)
LIMIT = 48 * 1024 * 1024
F32, BF16 = jnp.float32, jnp.bfloat16


def cost(us):
    return pl.CostEstimate(flops=0, bytes_accessed=int(us * 3.5e6), transcendentals=0)


def split2(x):
    hi = x.astype(BF16)
    lo = (x - hi.astype(F32)).astype(BF16)
    return hi, lo


def split3(x):
    hi = x.astype(BF16)
    rest = x - hi.astype(F32)
    mid = rest.astype(BF16)
    lo = (rest - mid.astype(F32)).astype(BF16)
    return hi, mid, lo


def times_nt(block, stacked):
    left = jnp.concatenate(split2(block), axis=0)
    full = lax.dot_general(left, stacked, (((1,), (1,)), ((), ())), preferred_element_type=F32)
    half = full[:K] + full[K:]
    return half[:, :TB] + half[:, TB:]


def times_nn(block, stacked):
    hi, lo = split2(block)
    left = jnp.concatenate(
        [jnp.concatenate([hi, hi], axis=1), jnp.concatenate([lo, lo], axis=1)], axis=0
    )
    full = lax.dot_general(left, stacked, (((1,), (0,)), ((), ())), preferred_element_type=F32)
    return full[:K] + full[K:]


def first_kernel(upos, item, tiles, lengths, panel, users, stacked):
    step = pl.program_id(0)

    @pl.when(step == 0)
    def _():
        users[...] = jnp.zeros_like(users)

    columns = lax.broadcasted_iota(jnp.int32, (TB, TB), 1)
    ends = lengths[...].T
    parts = []
    for t in range(GROUP):
        n = step * GROUP + t
        masked = jnp.where(columns < ends[:, t : t + 1], tiles[t], 0.0)
        both = jnp.concatenate(split2(masked), axis=0)
        stacked[t] = both
        block = panel[:, pl.ds(pl.multiple_of(item[n] * TB, TB), TB)]
        parts.append((upos[n], times_nt(block, both)))
    for spot, value in parts:
        users[spot] += value


def first_product(upos, item, tiles, lengths, panel_t):
    return pl.pallas_call(
        first_kernel,
        out_shape=(
            jax.ShapeDtypeStruct((UB, K, TB), F32),
            jax.ShapeDtypeStruct((NT, 2 * TB, TB), BF16),
        ),
        grid_spec=pltpu.PrefetchScalarGridSpec(
            num_scalar_prefetch=2,
            grid=(NT // GROUP,),
            in_specs=[
                pl.BlockSpec((GROUP, TB, TB), lambda s, *_: (s, 0, 0)),
                pl.BlockSpec((GROUP, TB), lambda s, *_: (s, 0)),
                pl.BlockSpec((K, IB * TB), lambda s, *_: (0, 0)),
            ],
            out_specs=[
                pl.BlockSpec((UB, K, TB), lambda s, *_: (0, 0, 0)),
                pl.BlockSpec((GROUP, 2 * TB, TB), lambda s, *_: (s, 0, 0)),
            ],
        ),
        cost_estimate=cost(13.8),
        compiler_params=pltpu.CompilerParams(vmem_limit_bytes=LIMIT),
    )(upos, item, tiles, lengths, panel_t)


def each_tile(first, last, lists, stacked, held, sems, total, use):
    start, end = lists[3 * NT + first], lists[3 * NT + last]
    steps = (end - start + RUN - 1) >> 4

    def begin(g, carry):
        for t in range(RUN):
            j = jnp.minimum(start + g * RUN + t, end - 1)
            pltpu.make_async_copy(stacked.at[lists[j]], held.at[g * RUN + t], sems.at[g]).start()
        return carry

    lax.fori_loop(0, steps, begin, 0)

    def step(g, carry):
        here = held.at[pl.ds(g * RUN, RUN)]
        pltpu.make_async_copy(stacked.at[pl.ds(0, RUN)], here, sems.at[g]).wait()
        parts = []
        for t in range(RUN):
            j = start + g * RUN + t
            at = jnp.minimum(j, end - 1)
            spot, value = use(lists[NT + at], lists[2 * NT + at], held[g * RUN + t])
            parts.append((spot, jnp.where(j < end, value, 0.0)))
        for spot, value in parts:
            total[spot] += value
        return carry

    lax.fori_loop(0, steps, step, 0)


def tile_scratch():
    return [pltpu.VMEM((NT, 2 * TB, TB), BF16), pltpu.SemaphoreType.DMA((NT // RUN,))]


def back_kernel(first, last, shift, sizes, lists, users, stacked, *rest):
    outs = rest[: len(sizes)]
    held, sems, total = rest[len(sizes) :]
    total[...] = jnp.zeros_like(total)

    def use(user, item, tile):
        return item - shift * HB, times_nn(users[user], tile)

    each_tile(first, last, lists, stacked, held, sems, total, use)
    at = 0
    for size, out in zip(sizes, outs):
        out[...] = total[at : at + size]
        at += size


def back_product(first, last, shift, sizes, lists, users, stacked):
    return pl.pallas_call(
        functools.partial(back_kernel, first, last, shift, sizes),
        out_shape=[jax.ShapeDtypeStruct((size, K, TB), F32) for size in sizes],
        in_specs=[SMEM, VMEM, ANY],
        out_specs=[VMEM] * len(sizes),
        scratch_shapes=tile_scratch() + [pltpu.VMEM((sum(sizes), K, TB), F32)],
        cost_estimate=cost(2.5 + 0.04 * sum(sizes)),
        compiler_params=pltpu.CompilerParams(vmem_limit_bytes=LIMIT),
    )(lists, users, stacked)


def forth_kernel(first, last, shift, cuts, more, lists, stacked, *rest):
    arrays = 1 + max(number for number, _ in cuts)
    ins = rest[:arrays]
    rest = rest[arrays:]
    if more:
        before, rest = rest[0], rest[1:]
    out, held, sems, panel = rest
    out[...] = before[...] if more else jnp.zeros_like(out)
    for place, (number, start) in enumerate(cuts):
        panel[place * HB : (place + 1) * HB] = ins[number][start : start + HB]

    def use(user, item, tile):
        return user, times_nt(panel[item - shift * HB], tile)

    each_tile(first, last, lists, stacked, held, sems, out, use)


def forth_product(first, last, shift, lists, stacked, arrays, cuts, before=None):
    more = before is not None
    args = list(arrays) + ([before] if more else [])
    return pl.pallas_call(
        functools.partial(forth_kernel, first, last, shift, cuts, more),
        out_shape=jax.ShapeDtypeStruct((UB, K, TB), F32),
        in_specs=[SMEM, ANY] + [VMEM] * len(args),
        out_specs=VMEM,
        scratch_shapes=tile_scratch() + [pltpu.VMEM((len(cuts) * HB, K, TB), F32)],
        cost_estimate=cost(3.0 + 0.5 * len(cuts)),
        compiler_params=pltpu.CompilerParams(vmem_limit_bytes=LIMIT),
    )(lists, stacked, *args)


def gram_kernel(own, out):
    total = jnp.zeros((3 * K, 3 * K), F32)
    for b in range(0, QB, 2):
        three = jnp.concatenate(split3(jnp.concatenate([own[b], own[b + 1]], axis=1)), axis=0)
        total += lax.dot_general(three, three, (((1,), (1,)), ((), ())), preferred_element_type=F32)
    rows = (total[2 * K :] + total[K : 2 * K]) + total[:K]
    out[...] = (rows[:, 2 * K :] + rows[:, K : 2 * K]) + rows[:, :K]


def gram_product(own):
    return pl.pallas_call(
        gram_kernel,
        out_shape=jax.ShapeDtypeStruct((K, K), F32),
        in_specs=[VMEM],
        out_specs=VMEM,
        cost_estimate=cost(0.7),
        compiler_params=pltpu.CompilerParams(vmem_limit_bytes=LIMIT),
    )(own)


def inverse_kernel(gram, out):
    rows = lax.broadcasted_iota(jnp.int32, (K, 2 * K), 0)
    lanes = lax.broadcasted_iota(jnp.int32, (K, 2 * K), 1)
    unit = (lanes == rows + K).astype(F32)
    left = gram[...] * F32(1.0 / ITEMS)
    work = jnp.concatenate([left, jnp.zeros((K, K), F32)], axis=1) + unit
    for k in range(K):
        pivot = work[k : k + 1, k : k + 1]
        scaled = work[k : k + 1, :] * lax.rsqrt(pivot)
        column = work[:, k : k + 1] * lax.rsqrt(pivot)
        lower = work - column * scaled
        work = jnp.where(rows > k, lower, jnp.where(rows == k, scaled, work))
    out[...] = work[:, K:]


def inverse_lower(gram):
    return pl.pallas_call(
        inverse_kernel,
        out_shape=jax.ShapeDtypeStruct((K, K), F32),
        in_specs=[VMEM],
        out_specs=VMEM,
        cost_estimate=cost(6.7),
    )(gram)


def exact_left(inverse):
    high, mid, low = split3(inverse)
    return jnp.concatenate([high, high, mid, mid], axis=1), jnp.concatenate([high, low], axis=1)


def exact_times(left, block):
    high, mid, low = split3(block)
    large = jnp.concatenate([high, mid, high, mid], axis=0)
    small = jnp.concatenate([low, high], axis=0)
    return jnp.dot(left[1], small, preferred_element_type=F32) + jnp.dot(
        left[0], large, preferred_element_type=F32
    )


def scale_kernel(inverse, users, out):
    left = exact_left(inverse[...])
    for b in range(UB):
        out[b] = exact_times(left, users[b])


def scale_users(inverse, users):
    return pl.pallas_call(
        scale_kernel,
        out_shape=jax.ShapeDtypeStruct((UB, K, TB), F32),
        in_specs=[VMEM] * 2,
        out_specs=VMEM,
        cost_estimate=cost(0.8),
        compiler_params=pltpu.CompilerParams(vmem_limit_bytes=LIMIT),
    )(inverse, users)


def final_kernel(cuts, base, inverse, *refs):
    out, made, sems = refs[-3:]
    left = exact_left(inverse[...])
    copies = []
    for place, (number, start) in enumerate(cuts):
        for b in range(HB):
            made[place, :, b * TB : (b + 1) * TB] = exact_times(left, refs[number][start + b])
        at = pl.multiple_of(base[place], HB * TB)
        copy = pltpu.make_async_copy(
            made.at[place], out.at[:, pl.ds(at, HB * TB)], sems.at[place]
        )
        copy.start()
        copies.append(copy)
    for copy in copies:
        copy.wait()


def final_product(base, inverse, arrays, cuts, before=None):
    more = [] if before is None else [before]
    return pl.pallas_call(
        functools.partial(final_kernel, cuts),
        out_shape=jax.ShapeDtypeStruct((K, IB * TB), F32),
        in_specs=[SMEM] + [VMEM] * (1 + len(arrays)) + [ANY] * len(more),
        out_specs=ANY,
        scratch_shapes=[
            pltpu.VMEM((len(cuts), K, HB * TB), F32),
            pltpu.SemaphoreType.DMA((len(cuts),)),
        ],
        input_output_aliases={2 + len(arrays): 0} if more else {},
        cost_estimate=cost(1.0 + 0.5 * len(cuts)),
        compiler_params=pltpu.CompilerParams(vmem_limit_bytes=LIMIT),
    )(base, inverse, *arrays, *more)


def user_move(value, by):
    return lax.ppermute(value, "user", [(s, (s + by) % 4) for s in range(4)])


def item_move(value, dy=0, dx=0, dc=0):
    pairs = []
    for y in range(4):
        for x in range(4):
            for c in range(2):
                to = (((y + dy) % 4) * 4 + (x + dx) % 4) * 2 + (c + dc) % 2
                pairs.append(((y * 4 + x) * 2 + c, to))
    return lax.ppermute(value, "item", pairs)


def sum_over_item(part):
    mine = part[:16] + item_move(part[16:], dc=1)
    near, right, far, left = mine[:4], mine[4:8], mine[8:12], mine[12:]
    mine = near + item_move(right, dx=1) + item_move(left, dx=-1) + item_move(far, dx=2)
    one, two, three = item_move(mine, dy=1), item_move(mine, dy=2), item_move(mine, dy=-1)
    mine = (mine + jnp.roll(two, 2, 0)) + (jnp.roll(one, -1, 0) + jnp.roll(three, 1, 0))
    left, far, right = item_move(mine, dx=1), item_move(mine, dx=2), item_move(mine, dx=-1)
    mine = jnp.concatenate([mine, right, far, left], axis=0)
    return jnp.concatenate([mine, item_move(mine, dc=1)], axis=0)


def sum_all_user(value):
    return (value + user_move(value, 2)) + (user_move(value, 1) + user_move(value, -1))


def sum_all_item(value):
    value = value + item_move(value, dc=1)
    value = (value + item_move(value, dx=2)) + (item_move(value, dx=1) + item_move(value, dx=-1))
    return (value + item_move(value, dy=2)) + (item_move(value, dy=1) + item_move(value, dy=-1))


FAR_A, FAR_B, UP_B, DOWN_A, UP_A, DOWN_B, OWN_A, OWN_B = range(8)
PLACES = {0: (OWN_A, OWN_B), 1: (UP_A, UP_B), 2: (FAR_A, FAR_B), 3: (DOWN_A, DOWN_B)}
BOUNDS = (0, UP_B, UP_A, OWN_A, 8)
OWN = ((0, 0), (0, HB))
NEAR = ((0, HB), (1, 0), (0, 0), (1, HB))
FAR = ((0, 0), (1, 0))


def cross_pieces(users, lists, stacked):
    far_a, far_b = back_product(0, 1, FAR_A, (HB, HB), lists, users, stacked)
    got_a, got_b = user_move(far_a, 1), user_move(far_b, -1)
    up_b, down_a = back_product(1, 2, UP_B, (HB, HB), lists, users, stacked)
    direct_b, direct_a = user_move(up_b, 1), user_move(down_a, -1)
    up_a, down_b, own = back_product(2, 4, UP_A, (HB, HB, QB), lists, users, stacked)
    sum_a, sum_b = user_move(up_a + got_a, 1), user_move(down_b + got_b, -1)
    own = own + jnp.concatenate([direct_a + sum_a, direct_b + sum_b], axis=0)
    down, up = user_move(own, 1), user_move(own, -1)
    gram = sum_all_user(sum_all_item(gram_product(own)))
    gram, down, up = lax.optimization_barrier((gram, down, up))
    far_a, far_b = user_move(down[:HB], 1), user_move(up[HB:], -1)
    return gram, (own,), (up, down), (far_a, far_b)


def tile_lists(upos, item_block, z):
    quarter = (item_block // QB - z) % 4
    half = (item_block // HB) % 2
    place = jnp.zeros_like(quarter)
    for at, (first, second) in PLACES.items():
        place = jnp.where(quarter == at, jnp.where(half == 0, first, second), place)
    ipos = place * HB + item_block % HB
    number = jnp.arange(NT, dtype=jnp.int32)
    key = ipos * NT + number
    rank = jnp.sum((key[None, :] < key[:, None]).astype(jnp.int32), axis=1)
    spot = rank[None, :] == number[:, None]

    def sort(values):
        return jnp.sum(jnp.where(spot, values[None, :], 0), axis=1)

    ends = jnp.array(BOUNDS, jnp.int32) * HB
    bounds = jnp.sum((ipos[None, :] < ends[:, None]).astype(jnp.int32), axis=1)
    return jnp.concatenate([sort(number), sort(upos), sort(ipos), bounds])


def body(tiles, tile_user, tile_item, row_lengths, start_panel):
    tiles = tiles.reshape(NT, TB, TB)
    user_block = tile_user.reshape(NT)
    item_block = tile_item.reshape(NT)
    spot = lax.axis_index("item")
    z = lax.axis_index("user")
    core, x, y = spot % 2, (spot // 2) % 4, spot // 8
    upos = ((user_block // 16) ^ core) * 16 + (((user_block // 4) % 4 - x) % 4) * 4 + (user_block % 4 - y) % 4

    part, stacked = first_product(upos, item_block, tiles, row_lengths.reshape(NT, TB), start_panel.T)
    lists = tile_lists(upos, item_block, z)
    users = sum_over_item(part)
    gram, own, near, far = cross_pieces(users, lists, stacked)
    part = forth_product(3, 4, OWN_A, lists, stacked, own, OWN)
    part = forth_product(1, 3, UP_B, lists, stacked, near, NEAR, part)
    part, inverse = lax.optimization_barrier((part, inverse_lower(gram)))
    part = forth_product(0, 1, FAR_A, lists, stacked, far, FAR, part)
    users = scale_users(inverse, sum_over_item(part))
    gram, own, near, far = cross_pieces(users, lists, stacked)
    inverse = inverse_lower(gram)
    halves = (0, 0), (0, 1), (1, 1), (3, 0), (1, 0), (3, 1), (2, 0), (2, 1)
    base = jnp.stack([((z + quarter) % 4) * (QB * TB) + half * (HB * TB) for quarter, half in halves])
    cuts = OWN + tuple((number + 1, at) for number, at in NEAR)
    panel = final_product(base[:6], inverse, own + near, cuts)
    return final_product(base[6:], inverse, far, FAR, panel).T


def solution(mesh):
    placed = (
        P("user", "item", None, None),
        P("user", "item"),
        P("user", "item"),
        P("user", "item", None),
        P("item", None),
    )
    return jax.shard_map(
        body, mesh=mesh, in_specs=placed, out_specs=P("item", None), check_vma=False
    )
```

```python
import functools

import jax
import jax.numpy as jnp
from jax import lax
from jax.experimental import pallas as pl
from jax.experimental.pallas import tpu as pltpu
from jax.sharding import PartitionSpec as P

ITERS = 2
TB = 128
K = 64
NT = 192
IB = 128
UB = 32
QB = 32
HB = 16
ITEMS = 524288
GROUP = 48
RUN = 16
VMEM = pl.BlockSpec(memory_space=pltpu.VMEM)
SMEM = pl.BlockSpec(memory_space=pltpu.SMEM)
ANY = pl.BlockSpec(memory_space=pl.ANY)
MIB = 1024 * 1024
F32, BF16 = jnp.float32, jnp.bfloat16


def cost(us):
    return pl.CostEstimate(flops=0, bytes_accessed=int(us * 3.5e6), transcendentals=0)


def split2(x):
    hi = x.astype(BF16)
    lo = (x - hi.astype(F32)).astype(BF16)
    return hi, lo


def split3(x):
    hi = x.astype(BF16)
    rest = x - hi.astype(F32)
    mid = rest.astype(BF16)
    lo = (rest - mid.astype(F32)).astype(BF16)
    return hi, mid, lo


def times_nt(block, stacked):
    left = jnp.concatenate(split2(block), axis=0)
    full = lax.dot_general(left, stacked, (((1,), (1,)), ((), ())), preferred_element_type=F32)
    half = full[:K] + full[K:]
    return half[:, :TB] + half[:, TB:]


def times_nn(block, stacked):
    hi, lo = split2(block)
    left = jnp.concatenate(
        [jnp.concatenate([hi, hi], axis=1), jnp.concatenate([lo, lo], axis=1)], axis=0
    )
    full = lax.dot_general(left, stacked, (((1,), (0,)), ((), ())), preferred_element_type=F32)
    return full[:K] + full[K:]


def place_of(user_block, spot):
    core = (user_block >> 4) ^ (spot & 1)
    x = ((user_block >> 2) - (spot >> 1)) & 3
    y = (user_block - (spot >> 3)) & 3
    return core * 16 + x * 4 + y


def first_kernel(upos, item, tiles, lengths, panel, users, stacked):
    step = pl.program_id(0)

    @pl.when(step == 0)
    def _():
        users[...] = jnp.zeros_like(users)

    columns = lax.broadcasted_iota(jnp.int32, (TB, TB), 1)
    ends = lengths[...].T
    parts = []
    for t in range(GROUP):
        n = step * GROUP + t
        masked = jnp.where(columns < ends[:, t : t + 1], tiles[t], 0.0)
        both = jnp.concatenate(split2(masked), axis=0)
        stacked[t] = both
        block = panel[:, pl.ds(pl.multiple_of(item[n] * TB, TB), TB)]
        parts.append((upos[n], times_nt(block, both)))
    for spot, value in parts:
        users[spot] += value


def first_product(upos, item, tiles, lengths, panel_t):
    return pl.pallas_call(
        first_kernel,
        out_shape=(
            jax.ShapeDtypeStruct((UB, K, TB), F32),
            pltpu.VMEM((NT, 2 * TB, TB), BF16),
        ),
        grid_spec=pltpu.PrefetchScalarGridSpec(
            num_scalar_prefetch=2,
            grid=(NT // GROUP,),
            in_specs=[
                pl.BlockSpec((GROUP, TB, TB), lambda s, *_: (s, 0, 0)),
                pl.BlockSpec((GROUP, TB), lambda s, *_: (s, 0)),
                pl.BlockSpec((K, IB * TB), lambda s, *_: (0, 0)),
            ],
            out_specs=[
                pl.BlockSpec((UB, K, TB), lambda s, *_: (0, 0, 0)),
                pl.BlockSpec((GROUP, 2 * TB, TB), lambda s, *_: (s, 0, 0)),
            ],
        ),
        cost_estimate=cost(13.8),
        compiler_params=pltpu.CompilerParams(vmem_limit_bytes=28 * MIB),
    )(upos, item, tiles, lengths, panel_t)


def each_tile(first, last, lists, stacked, total, use):
    start, end = lists[3 * NT + first], lists[3 * NT + last]

    def step(g, carry):
        parts = []
        for t in range(RUN):
            j = start + g * RUN + t
            at = jnp.minimum(j, end - 1)
            spot, value = use(lists[NT + at], lists[2 * NT + at], stacked[lists[at]])
            parts.append((spot, jnp.where(j < end, value, 0.0)))
        for spot, value in parts:
            total[spot, :K] += value
        return carry

    lax.fori_loop(0, (end - start + RUN - 1) >> 4, step, 0)


def back_kernel(first, last, shift, sizes, lists, users, stacked, *rest):
    outs = rest[: len(sizes)]
    (total,) = rest[len(sizes) :]
    total[...] = jnp.zeros_like(total)

    def use(user, item, tile):
        return item - shift * HB, times_nn(users[user, :K], tile)

    each_tile(first, last, lists, stacked, total, use)
    at = 0
    for size, out in zip(sizes, outs):
        out[...] = total[at : at + size]
        at += size


def back_product(first, last, shift, sizes, lists, users, stacked):
    return pl.pallas_call(
        functools.partial(back_kernel, first, last, shift, sizes),
        out_shape=[jax.ShapeDtypeStruct((size, K, TB), F32) for size in sizes],
        in_specs=[SMEM, VMEM, VMEM],
        out_specs=[VMEM] * len(sizes),
        scratch_shapes=[pltpu.VMEM((sum(sizes), K, TB), F32)],
        cost_estimate=cost(2.5 + 0.04 * sum(sizes)),
        compiler_params=pltpu.CompilerParams(vmem_limit_bytes=8 * MIB),
    )(lists, users, stacked)


def gram_of(blocks):
    total = jnp.zeros((3 * K, 3 * K), F32)
    for first, second in zip(blocks[::2], blocks[1::2]):
        three = jnp.concatenate(split3(jnp.concatenate([first, second], axis=1)), axis=0)
        total += lax.dot_general(three, three, (((1,), (1,)), ((), ())), preferred_element_type=F32)
    rows = (total[2 * K :] + total[K : 2 * K]) + total[:K]
    return (rows[:, 2 * K :] + rows[:, K : 2 * K]) + rows[:, :K]


def forth_kernel(first, last, shift, count, more, final, lists, stacked, *rest):
    ins = rest[:count]
    rest = rest[count:]
    if more:
        before, gram_before, rest = rest[0], rest[1], rest[2:]
    if final:
        out, panel = rest
        out[...] = jnp.zeros_like(out)
    else:
        out, gram, panel = rest
    out[:, :K] = before[...] if more else jnp.zeros((UB, K, TB), F32)
    for place, piece in enumerate(ins):
        panel[place * HB : (place + 1) * HB] = piece[...]

    def use(user, item, tile):
        return user, times_nt(panel[item - shift * HB], tile)

    own = gram_of([panel[b] for b in range(count * HB)])
    if more:
        own = own + gram_before[...]
    if final:
        for b in range(UB):
            out[lists[PLACE_AT + b], K : K + 2, :K] = own[2 * b : 2 * b + 2]
    else:
        gram[...] = own
    each_tile(first, last, lists, stacked, out, use)


def forth_product(first, last, shift, lists, stacked, pieces, before=None, final=False):
    more = before is not None
    args = list(pieces) + (list(before) if more else [])
    shapes = [jax.ShapeDtypeStruct((UB, K, TB), F32), jax.ShapeDtypeStruct((K, K), F32)]
    if final:
        shapes = [jax.ShapeDtypeStruct((UB, K + 8, TB), F32)]
    return pl.pallas_call(
        functools.partial(forth_kernel, first, last, shift, len(pieces), more, final),
        out_shape=shapes,
        in_specs=[SMEM] + [VMEM] * (1 + len(args)),
        out_specs=[VMEM] * len(shapes),
        scratch_shapes=[pltpu.VMEM((len(pieces) * HB, K, TB), F32)],
        cost_estimate=cost(3.0 + 0.8 * len(pieces)),
        compiler_params=pltpu.CompilerParams(vmem_limit_bytes=8 * MIB),
    )(lists, stacked, *args)


def gram_kernel(own, out):
    out[...] = gram_of([own[b] for b in range(QB)])


def gram_product(own):
    return pl.pallas_call(
        gram_kernel,
        out_shape=jax.ShapeDtypeStruct((K, K), F32),
        in_specs=[VMEM],
        out_specs=VMEM,
        cost_estimate=cost(0.7),
        compiler_params=pltpu.CompilerParams(vmem_limit_bytes=4 * MIB),
    )(own)


def inverse_of(gram):
    rows = lax.broadcasted_iota(jnp.int32, (K, 2 * K), 0)
    lanes = lax.broadcasted_iota(jnp.int32, (K, 2 * K), 1)
    unit = (lanes == rows + K).astype(F32)
    left = gram * F32(1.0 / ITEMS)
    work = jnp.concatenate([left, jnp.zeros((K, K), F32)], axis=1) + unit
    for k in range(K):
        pivot = work[k : k + 1, k : k + 1]
        scaled = work[k : k + 1, :] * lax.rsqrt(pivot)
        column = work[:, k : k + 1] * lax.rsqrt(pivot)
        lower = work - column * scaled
        work = jnp.where(rows > k, lower, jnp.where(rows == k, scaled, work))
    return work[:, K:]


def inverse_kernel(gram, out):
    out[...] = inverse_of(gram[...])


def inverse_lower(gram):
    return pl.pallas_call(
        inverse_kernel,
        out_shape=jax.ShapeDtypeStruct((K, K), F32),
        in_specs=[VMEM],
        out_specs=VMEM,
        cost_estimate=cost(6.7),
        compiler_params=pltpu.CompilerParams(vmem_limit_bytes=2 * MIB),
    )(gram)


def inverse_beside_kernel(lists, users, out, gram):
    for b in range(UB):
        gram[2 * b : 2 * b + 2] = users[lists[PLACE_AT + b], K : K + 2, :K]
    out[...] = inverse_of(gram[...])


def inverse_beside(lists, users):
    return pl.pallas_call(
        inverse_beside_kernel,
        out_shape=jax.ShapeDtypeStruct((K, K), F32),
        in_specs=[SMEM, VMEM],
        out_specs=VMEM,
        scratch_shapes=[pltpu.VMEM((K, K), F32)],
        cost_estimate=cost(6.9),
        compiler_params=pltpu.CompilerParams(vmem_limit_bytes=2 * MIB),
    )(lists, users)


def exact_left(inverse):
    high, mid, low = split3(inverse)
    return jnp.concatenate([high, high, mid, mid], axis=1), jnp.concatenate([high, low], axis=1)


def exact_times(left, block):
    high, mid, low = split3(block)
    large = jnp.concatenate([high, mid, high, mid], axis=0)
    small = jnp.concatenate([low, high], axis=0)
    return jnp.dot(left[1], small, preferred_element_type=F32) + jnp.dot(
        left[0], large, preferred_element_type=F32
    )


def scale_kernel(inverse, *refs):
    left = exact_left(inverse[...])
    out = refs[-1]
    for half in range(2):
        first, second, third = refs[3 * half : 3 * half + 3]
        for b in range(HB):
            out[half * HB + b] = exact_times(left, (first[b] + second[b]) + third[b])


def scale_sum(inverse, terms):
    return pl.pallas_call(
        scale_kernel,
        out_shape=jax.ShapeDtypeStruct((QB, K, TB), F32),
        in_specs=[VMEM] * 7,
        out_specs=VMEM,
        cost_estimate=cost(0.9),
        compiler_params=pltpu.CompilerParams(vmem_limit_bytes=4 * MIB),
    )(inverse, *terms)


def final_kernel(cuts, base, inverse, *refs):
    out, made, sems = refs[-3:]
    left = exact_left(inverse[...])
    copies = []
    for place, (number, start) in enumerate(cuts):
        for b in range(HB):
            made[place, :, b * TB : (b + 1) * TB] = exact_times(left, refs[number][start + b])
        at = pl.multiple_of(base[place], HB * TB)
        copy = pltpu.make_async_copy(
            made.at[place], out.at[:, pl.ds(at, HB * TB)], sems.at[place]
        )
        copy.start()
        copies.append(copy)
    for copy in copies:
        copy.wait()


def final_product(base, inverse, arrays, cuts, before=None):
    more = [] if before is None else [before]
    return pl.pallas_call(
        functools.partial(final_kernel, cuts),
        out_shape=jax.ShapeDtypeStruct((K, IB * TB), F32),
        in_specs=[SMEM] + [VMEM] * (1 + len(arrays)) + [ANY] * len(more),
        out_specs=ANY,
        scratch_shapes=[
            pltpu.VMEM((len(cuts), K, HB * TB), F32),
            pltpu.SemaphoreType.DMA((len(cuts),)),
        ],
        input_output_aliases={2 + len(arrays): 0} if more else {},
        cost_estimate=cost(1.0 + 0.5 * len(cuts)),
        compiler_params=pltpu.CompilerParams(vmem_limit_bytes=8 * MIB),
    )(base, inverse, *arrays, *more)


def user_move(value, by):
    return lax.ppermute(value, "user", [(s, (s + by) % 4) for s in range(4)])


def item_move(value, dy=0, dx=0, dc=0):
    pairs = []
    for y in range(4):
        for x in range(4):
            for c in range(2):
                to = (((y + dy) % 4) * 4 + (x + dx) % 4) * 2 + (c + dc) % 2
                pairs.append(((y * 4 + x) * 2 + c, to))
    return lax.ppermute(value, "item", pairs)


def sum_over_item(part):
    mine = part[:16] + item_move(part[16:], dc=1)
    near, right, far, left = mine[:4], mine[4:8], mine[8:12], mine[12:]
    mine = near + item_move(right, dx=1) + item_move(left, dx=-1) + item_move(far, dx=2)
    one, two, three = item_move(mine, dy=1), item_move(mine, dy=2), item_move(mine, dy=-1)
    mine = (mine + jnp.roll(two, 2, 0)) + (jnp.roll(one, -1, 0) + jnp.roll(three, 1, 0))
    left, far, right = item_move(mine, dx=1), item_move(mine, dx=2), item_move(mine, dx=-1)
    mine = jnp.concatenate([mine, right, far, left], axis=0)
    return jnp.concatenate([mine, item_move(mine, dc=1)], axis=0)


def sum_all_user(value):
    return (value + user_move(value, 2)) + (user_move(value, 1) + user_move(value, -1))


def sum_all_item(value):
    value = value + item_move(value, dc=1)
    value = (value + item_move(value, dx=2)) + (item_move(value, dx=1) + item_move(value, dx=-1))
    return (value + item_move(value, dy=2)) + (item_move(value, dy=1) + item_move(value, dy=-1))


FAR_A, FAR_B, UP_B, DOWN_A, UP_A, DOWN_B, OWN_A, OWN_B = range(8)
PLACES = {0: (OWN_A, OWN_B), 1: (UP_A, UP_B), 2: (FAR_A, FAR_B), 3: (DOWN_A, DOWN_B)}
BOUNDS = (0, UP_B, UP_A, OWN_A, 8)
PLACE_AT = 3 * NT + len(BOUNDS)
LISTS = 640


def scatter(users, lists, stacked):
    far_a, far_b = back_product(0, 1, FAR_A, (HB, HB), lists, users, stacked)
    got_a, got_b = user_move(far_a, 1), user_move(far_b, -1)
    up_b, down_a = back_product(1, 2, UP_B, (HB, HB), lists, users, stacked)
    direct_b, direct_a = user_move(up_b, 1), user_move(down_a, -1)
    up_a, down_b, own_a, own_b = back_product(2, 4, UP_A, (HB,) * 4, lists, users, stacked)
    sum_a, sum_b = user_move(up_a + got_a, 1), user_move(down_b + got_b, -1)
    return lax.optimization_barrier((own_a, direct_a, sum_a, own_b, direct_b, sum_b))


def item_places(item_block, z):
    quarter = (item_block // QB - z) % 4
    half = (item_block // HB) % 2
    place = jnp.zeros_like(quarter)
    for at, (first, second) in PLACES.items():
        place = jnp.where(quarter == at, jnp.where(half == 0, first, second), place)
    return place * HB + item_block % HB


def tile_lists(upos, ipos, places):
    number = jnp.arange(NT, dtype=jnp.int32)
    key = ipos * NT + number
    rank = jnp.sum((key[None, :] < key[:, None]).astype(jnp.int32), axis=1)
    spot = rank[None, :] == number[:, None]

    def sort(values):
        return jnp.sum(jnp.where(spot, values[None, :], 0), axis=1)

    ends = jnp.array(BOUNDS, jnp.int32) * HB
    bounds = jnp.sum((ipos[None, :] < ends[:, None]).astype(jnp.int32), axis=1)
    out = jnp.zeros((LISTS,), jnp.int32)
    at = 0
    for piece in (sort(number), sort(upos), sort(ipos), bounds, places):
        out = out + jnp.pad(piece, (at, LISTS - at - piece.shape[0]))
        at += piece.shape[0]
    return out


def body(tiles, tile_user, tile_item, row_lengths, start_panel):
    tiles = tiles.reshape(NT, TB, TB)
    user_block = tile_user.reshape(NT)
    item_block = tile_item.reshape(NT)
    spot = lax.axis_index("item")
    z = lax.axis_index("user")

    halves = (0, 0), (0, 1), (3, 0), (3, 1), (1, 0), (1, 1), (2, 0), (2, 1)
    quarters, odd = (jnp.array(column, jnp.int32) for column in zip(*halves))
    base = ((z + quarters) % 4) * (QB * TB) + odd * (HB * TB)
    upos, places = place_of(user_block, spot), place_of(jnp.arange(UB, dtype=jnp.int32), spot)
    ipos = item_places(item_block, z)
    upos, ipos, places, base = lax.optimization_barrier((upos, ipos, places, base))
    part, stacked = first_product(upos, item_block, tiles, row_lengths.reshape(NT, TB), start_panel.T)
    lists = tile_lists(upos, ipos, places)
    users = sum_over_item(part)
    terms = scatter(users, lists, stacked)
    own_a, own_b = (terms[0] + terms[1]) + terms[2], (terms[3] + terms[4]) + terms[5]
    down_a, up_b = user_move(own_a, 1), user_move(own_b, -1)
    down_b, up_a = user_move(own_b, 1), user_move(own_a, -1)
    far = user_move(down_a, 1), user_move(up_b, -1)
    before = forth_product(3, 4, OWN_A, lists, stacked, (own_a, own_b))
    before = forth_product(1, 3, UP_B, lists, stacked, (up_b, down_a, up_a, down_b), before)
    (part,) = forth_product(0, 1, FAR_A, lists, stacked, far, before, True)
    users = sum_over_item(part)
    terms = scatter(users, lists, stacked)
    own = scale_sum(inverse_beside(lists, users), terms)
    down, up = user_move(own, 1), user_move(own, -1)
    gram = sum_all_user(sum_all_item(gram_product(own)))
    gram, down, up = lax.optimization_barrier((gram, down, up))
    far = user_move(down[:HB], 1), user_move(up[HB:], -1)
    inverse = inverse_lower(gram)
    cuts = (0, 0), (0, HB), (1, 0), (1, HB), (2, 0), (2, HB)
    panel = final_product(base[:6], inverse, (own, down, up), cuts)
    return final_product(base[6:], inverse, far, ((0, 0), (1, 0)), panel).T


def solution(mesh):
    placed = (
        P("user", "item", None, None),
        P("user", "item"),
        P("user", "item"),
        P("user", "item", None),
        P("item", None),
    )
    return jax.shard_map(
        body, mesh=mesh, in_specs=placed, out_specs=P("item", None), check_vma=False
    )
```

```python
import functools

import jax
import jax.numpy as jnp
from jax import lax
from jax.experimental import pallas as pl
from jax.experimental.pallas import tpu as pltpu
from jax.sharding import PartitionSpec as P

ITERS = 2
TB = 128
K = 64
NT = 192
IB = 128
UB = 32
QB = 32
HB = 16
ITEMS = 524288
GROUP = 48
RUN = 16
VMEM = pl.BlockSpec(memory_space=pltpu.VMEM)
SMEM = pl.BlockSpec(memory_space=pltpu.SMEM)
ANY = pl.BlockSpec(memory_space=pl.ANY)
MIB = 1024 * 1024
F32, BF16 = jnp.float32, jnp.bfloat16


def cost(us):
    return pl.CostEstimate(flops=0, bytes_accessed=int(us * 3.5e6), transcendentals=0)


def split2(x):
    hi = x.astype(BF16)
    lo = (x - hi.astype(F32)).astype(BF16)
    return hi, lo


def split3(x):
    hi = x.astype(BF16)
    rest = x - hi.astype(F32)
    mid = rest.astype(BF16)
    lo = (rest - mid.astype(F32)).astype(BF16)
    return hi, mid, lo


def times_nt(block, stacked):
    left = jnp.concatenate(split2(block), axis=0)
    full = lax.dot_general(left, stacked, (((1,), (1,)), ((), ())), preferred_element_type=F32)
    half = full[:K] + full[K:]
    return half[:, :TB] + half[:, TB:]


def times_nn(block, stacked):
    hi, lo = split2(block)
    left = jnp.concatenate(
        [jnp.concatenate([hi, hi], axis=1), jnp.concatenate([lo, lo], axis=1)], axis=0
    )
    full = lax.dot_general(left, stacked, (((1,), (0,)), ((), ())), preferred_element_type=F32)
    return full[:K] + full[K:]


def place_of(user_block, spot):
    core = (user_block >> 4) ^ (spot & 1)
    x = ((user_block >> 2) - (spot >> 1)) & 3
    y = (user_block - (spot >> 3)) & 3
    return core * 16 + x * 4 + y


def first_kernel(tiles, user_in, item_in, lengths_in, panel_in, users, stacked, where, user, item, lengths, panel, sems):
    step = pl.program_id(0)
    spot = lax.axis_index("item")

    @pl.when(step == 0)
    def _():
        pairs = (panel_in, panel), (lengths_in, lengths), (user_in, user), (item_in, item)
        copies = [
            pltpu.make_async_copy(source, target, sems.at[number])
            for number, (source, target) in enumerate(pairs)
        ]
        for copy in copies:
            copy.start()
        users[...] = jnp.zeros_like(users)
        rows = lax.broadcasted_iota(jnp.int32, where.shape, 0)
        where[...] = jnp.where(rows == 0, spot, lax.axis_index("user"))
        for copy in copies:
            copy.wait()

    columns = lax.broadcasted_iota(jnp.int32, (TB, TB), 1)
    ends = lengths[pl.ds(pl.multiple_of(step * GROUP, GROUP), GROUP)].T
    parts = []
    for t in range(GROUP):
        n = step * GROUP + t
        masked = jnp.where(columns < ends[:, t : t + 1], tiles[t], 0.0)
        both = jnp.concatenate(split2(masked), axis=0)
        stacked[t] = both
        block = panel[:, pl.ds(pl.multiple_of(item[n] * TB, TB), TB)]
        parts.append((place_of(user[n], spot), times_nt(block, both)))
    for at, value in parts:
        users[at] += value


def first_product(user, item, tiles, lengths, panel_t):
    return pl.pallas_call(
        first_kernel,
        out_shape=(
            jax.ShapeDtypeStruct((UB, K, TB), F32),
            jax.ShapeDtypeStruct((NT, 2 * TB, TB), BF16),
            jax.ShapeDtypeStruct((8, 2 * TB), jnp.int32),
        ),
        grid=(NT // GROUP,),
        in_specs=[pl.BlockSpec((GROUP, TB, TB), lambda s: (s, 0, 0))]
        + [pl.BlockSpec(memory_space=pltpu.HBM)] * 4,
        out_specs=[
            pl.BlockSpec((UB, K, TB), lambda s: (0, 0, 0)),
            pl.BlockSpec((GROUP, 2 * TB, TB), lambda s: (s, 0, 0)),
            pl.BlockSpec((8, 2 * TB), lambda s: (0, 0)),
        ],
        scratch_shapes=[
            pltpu.SMEM((NT,), jnp.int32),
            pltpu.SMEM((NT,), jnp.int32),
            pltpu.VMEM((NT, TB), jnp.int32),
            pltpu.VMEM((K, IB * TB), F32),
            pltpu.SemaphoreType.DMA((4,)),
        ],
        cost_estimate=cost(10.0),
        compiler_params=pltpu.CompilerParams(vmem_limit_bytes=28 * MIB),
    )(*(pltpu.with_memory_space_constraint(x, pltpu.HBM) for x in (tiles, user, item, lengths, panel_t)))


def each_tile(first, last, lists, stacked, total, use):
    start, end = lists[3 * NT + first], lists[3 * NT + last]

    def step(g, carry):
        parts = []
        for t in range(RUN):
            j = start + g * RUN + t
            at = jnp.minimum(j, end - 1)
            spot, value = use(lists[NT + at], lists[2 * NT + at], stacked[lists[at]])
            parts.append((spot, jnp.where(j < end, value, 0.0)))
        for spot, value in parts:
            total[spot, :K] += value
        return carry

    lax.fori_loop(0, (end - start + RUN - 1) >> 4, step, 0)


def back_kernel(first, last, shift, sizes, lists, users, stacked, *rest):
    outs = rest[: len(sizes)]
    (total,) = rest[len(sizes) :]
    total[...] = jnp.zeros_like(total)

    def use(user, item, tile):
        return item - shift * HB, times_nn(users[user, :K], tile)

    each_tile(first, last, lists, stacked, total, use)
    at = 0
    for size, out in zip(sizes, outs):
        out[...] = total[at : at + size]
        at += size


def back_product(first, last, shift, sizes, lists, users, stacked):
    return pl.pallas_call(
        functools.partial(back_kernel, first, last, shift, sizes),
        out_shape=[jax.ShapeDtypeStruct((size, K, TB), F32) for size in sizes],
        in_specs=[SMEM, VMEM, VMEM],
        out_specs=[VMEM] * len(sizes),
        scratch_shapes=[pltpu.VMEM((sum(sizes), K, TB), F32)],
        cost_estimate=cost(2.5 + 0.04 * sum(sizes)),
        compiler_params=pltpu.CompilerParams(vmem_limit_bytes=8 * MIB),
    )(lists, users, stacked)


def gram_of(blocks):
    total = jnp.zeros((3 * K, 3 * K), F32)
    for first, second in zip(blocks[::2], blocks[1::2]):
        three = jnp.concatenate(split3(jnp.concatenate([first, second], axis=1)), axis=0)
        total += lax.dot_general(three, three, (((1,), (1,)), ((), ())), preferred_element_type=F32)
    rows = (total[2 * K :] + total[K : 2 * K]) + total[:K]
    return (rows[:, 2 * K :] + rows[:, K : 2 * K]) + rows[:, :K]


def forth_kernel(first, last, shift, count, more, final, lists, stacked, *rest):
    ins = rest[:count]
    rest = rest[count:]
    if more:
        before, gram_before, rest = rest[0], rest[1], rest[2:]
    if final:
        out, panel = rest
        out[...] = jnp.zeros_like(out)
    else:
        out, gram, panel = rest
    out[:, :K] = before[...] if more else jnp.zeros((UB, K, TB), F32)
    for place, piece in enumerate(ins):
        panel[place * HB : (place + 1) * HB] = piece[...]

    def use(user, item, tile):
        return user, times_nt(panel[item - shift * HB], tile)

    own = gram_of([panel[b] for b in range(count * HB)])
    if more:
        own = own + gram_before[...]
    if final:
        for b in range(UB):
            out[lists[PLACE_AT + b], K : K + 2, :K] = own[2 * b : 2 * b + 2]
    else:
        gram[...] = own
    each_tile(first, last, lists, stacked, out, use)


def forth_product(first, last, shift, lists, stacked, pieces, before=None, final=False):
    more = before is not None
    args = list(pieces) + (list(before) if more else [])
    shapes = [jax.ShapeDtypeStruct((UB, K, TB), F32), jax.ShapeDtypeStruct((K, K), F32)]
    if final:
        shapes = [jax.ShapeDtypeStruct((UB, K + 8, TB), F32)]
    return pl.pallas_call(
        functools.partial(forth_kernel, first, last, shift, len(pieces), more, final),
        out_shape=shapes,
        in_specs=[SMEM] + [VMEM] * (1 + len(args)),
        out_specs=[VMEM] * len(shapes),
        scratch_shapes=[pltpu.VMEM((len(pieces) * HB, K, TB), F32)],
        cost_estimate=cost(3.0 + 0.8 * len(pieces)),
        compiler_params=pltpu.CompilerParams(vmem_limit_bytes=8 * MIB),
    )(lists, stacked, *args)


def gram_kernel(own, out):
    out[...] = gram_of([own[b] for b in range(QB)])


def gram_product(own):
    return pl.pallas_call(
        gram_kernel,
        out_shape=jax.ShapeDtypeStruct((K, K), F32),
        in_specs=[VMEM],
        out_specs=VMEM,
        cost_estimate=cost(0.7),
        compiler_params=pltpu.CompilerParams(vmem_limit_bytes=4 * MIB),
    )(own)


def inverse_of(gram):
    rows = lax.broadcasted_iota(jnp.int32, (K, 2 * K), 0)
    lanes = lax.broadcasted_iota(jnp.int32, (K, 2 * K), 1)
    unit = (lanes == rows + K).astype(F32)
    left = gram * F32(1.0 / ITEMS)
    work = jnp.concatenate([left, jnp.zeros((K, K), F32)], axis=1) + unit
    for k in range(K):
        pivot = work[k : k + 1, k : k + 1]
        scaled = work[k : k + 1, :] * lax.rsqrt(pivot)
        column = work[:, k : k + 1] * lax.rsqrt(pivot)
        lower = work - column * scaled
        work = jnp.where(rows > k, lower, jnp.where(rows == k, scaled, work))
    return work[:, K:]


def inverse_kernel(gram, out):
    out[...] = inverse_of(gram[...])


def inverse_lower(gram):
    return pl.pallas_call(
        inverse_kernel,
        out_shape=jax.ShapeDtypeStruct((K, K), F32),
        in_specs=[VMEM],
        out_specs=VMEM,
        cost_estimate=cost(6.7),
        compiler_params=pltpu.CompilerParams(vmem_limit_bytes=2 * MIB),
    )(gram)


def inverse_beside_kernel(lists, users, out, gram):
    for b in range(UB):
        gram[2 * b : 2 * b + 2] = users[lists[PLACE_AT + b], K : K + 2, :K]
    out[...] = inverse_of(gram[...])


def inverse_beside(lists, users):
    return pl.pallas_call(
        inverse_beside_kernel,
        out_shape=jax.ShapeDtypeStruct((K, K), F32),
        in_specs=[SMEM, VMEM],
        out_specs=VMEM,
        scratch_shapes=[pltpu.VMEM((K, K), F32)],
        cost_estimate=cost(6.9),
        compiler_params=pltpu.CompilerParams(vmem_limit_bytes=2 * MIB),
    )(lists, users)


def exact_left(inverse):
    high, mid, low = split3(inverse)
    return jnp.concatenate([high, high, mid, mid], axis=1), jnp.concatenate([high, low], axis=1)


def exact_times(left, block):
    high, mid, low = split3(block)
    large = jnp.concatenate([high, mid, high, mid], axis=0)
    small = jnp.concatenate([low, high], axis=0)
    return jnp.dot(left[1], small, preferred_element_type=F32) + jnp.dot(
        left[0], large, preferred_element_type=F32
    )


def scale_kernel(inverse, *refs):
    left = exact_left(inverse[...])
    out = refs[-1]
    for half in range(2):
        first, second, third = refs[3 * half : 3 * half + 3]
        for b in range(HB):
            out[half * HB + b] = exact_times(left, (first[b] + second[b]) + third[b])


def scale_sum(inverse, terms):
    return pl.pallas_call(
        scale_kernel,
        out_shape=jax.ShapeDtypeStruct((QB, K, TB), F32),
        in_specs=[VMEM] * 7,
        out_specs=VMEM,
        cost_estimate=cost(0.9),
        compiler_params=pltpu.CompilerParams(vmem_limit_bytes=4 * MIB),
    )(inverse, *terms)


def final_kernel(cuts, base, inverse, *refs):
    out, made, sems = refs[-3:]
    left = exact_left(inverse[...])
    copies = []
    for place, (number, start) in enumerate(cuts):
        for b in range(HB):
            made[place, :, b * TB : (b + 1) * TB] = exact_times(left, refs[number][start + b])
        at = pl.multiple_of(base[place], HB * TB)
        copy = pltpu.make_async_copy(
            made.at[place], out.at[:, pl.ds(at, HB * TB)], sems.at[place]
        )
        copy.start()
        copies.append(copy)
    for copy in copies:
        copy.wait()


def final_product(base, inverse, arrays, cuts, before=None):
    more = [] if before is None else [before]
    return pl.pallas_call(
        functools.partial(final_kernel, cuts),
        out_shape=jax.ShapeDtypeStruct((K, IB * TB), F32),
        in_specs=[SMEM] + [VMEM] * (1 + len(arrays)) + [ANY] * len(more),
        out_specs=ANY,
        scratch_shapes=[
            pltpu.VMEM((len(cuts), K, HB * TB), F32),
            pltpu.SemaphoreType.DMA((len(cuts),)),
        ],
        input_output_aliases={2 + len(arrays): 0} if more else {},
        cost_estimate=cost(1.0 + 0.5 * len(cuts)),
        compiler_params=pltpu.CompilerParams(vmem_limit_bytes=8 * MIB),
    )(base, inverse, *arrays, *more)


def user_move(value, by):
    return lax.ppermute(value, "user", [(s, (s + by) % 4) for s in range(4)])


def item_move(value, dy=0, dx=0, dc=0):
    pairs = []
    for y in range(4):
        for x in range(4):
            for c in range(2):
                to = (((y + dy) % 4) * 4 + (x + dx) % 4) * 2 + (c + dc) % 2
                pairs.append(((y * 4 + x) * 2 + c, to))
    return lax.ppermute(value, "item", pairs)


def sum_over_item(part):
    mine = part[:16] + item_move(part[16:], dc=1)
    near, right, far, left = mine[:4], mine[4:8], mine[8:12], mine[12:]
    mine = near + item_move(right, dx=1) + item_move(left, dx=-1) + item_move(far, dx=2)
    one, two, three = item_move(mine, dy=1), item_move(mine, dy=2), item_move(mine, dy=-1)
    mine = (mine + jnp.roll(two, 2, 0)) + (jnp.roll(one, -1, 0) + jnp.roll(three, 1, 0))
    left, far, right = item_move(mine, dx=1), item_move(mine, dx=2), item_move(mine, dx=-1)
    mine = jnp.concatenate([mine, right, far, left], axis=0)
    return jnp.concatenate([mine, item_move(mine, dc=1)], axis=0)


def sum_all_user(value):
    return (value + user_move(value, 2)) + (user_move(value, 1) + user_move(value, -1))


def sum_all_item(value):
    value = value + item_move(value, dc=1)
    value = (value + item_move(value, dx=2)) + (item_move(value, dx=1) + item_move(value, dx=-1))
    return (value + item_move(value, dy=2)) + (item_move(value, dy=1) + item_move(value, dy=-1))


FAR_A, FAR_B, UP_B, DOWN_A, UP_A, DOWN_B, OWN_A, OWN_B = range(8)
PLACES = {0: (OWN_A, OWN_B), 1: (UP_A, UP_B), 2: (FAR_A, FAR_B), 3: (DOWN_A, DOWN_B)}
BOUNDS = (0, UP_B, UP_A, OWN_A, 8)
PLACE_AT = 3 * NT + len(BOUNDS)
LISTS = 640


def scatter(users, lists, stacked):
    far_a, far_b = back_product(0, 1, FAR_A, (HB, HB), lists, users, stacked)
    got_a, got_b = user_move(far_a, 1), user_move(far_b, -1)
    up_b, down_a = back_product(1, 2, UP_B, (HB, HB), lists, users, stacked)
    direct_b, direct_a = user_move(up_b, 1), user_move(down_a, -1)
    up_a, down_b, own_a, own_b = back_product(2, 4, UP_A, (HB,) * 4, lists, users, stacked)
    sum_a, sum_b = user_move(up_a + got_a, 1), user_move(down_b + got_b, -1)
    return lax.optimization_barrier((own_a, direct_a, sum_a, own_b, direct_b, sum_b))


def item_places(item_block, z):
    quarter = (item_block // QB - z) % 4
    half = (item_block // HB) % 2
    place = jnp.zeros_like(quarter)
    for at, (first, second) in PLACES.items():
        place = jnp.where(quarter == at, jnp.where(half == 0, first, second), place)
    return place * HB + item_block % HB


def tile_lists(upos, ipos, places):
    number = jnp.arange(NT, dtype=jnp.int32)
    key = ipos * NT + number
    rank = jnp.sum((key[None, :] < key[:, None]).astype(jnp.int32), axis=1)
    spot = rank[None, :] == number[:, None]

    def sort(values):
        return jnp.sum(jnp.where(spot, values[None, :], 0), axis=1)

    ends = jnp.array(BOUNDS, jnp.int32) * HB
    bounds = jnp.sum((ipos[None, :] < ends[:, None]).astype(jnp.int32), axis=1)
    out = jnp.zeros((LISTS,), jnp.int32)
    at = 0
    for piece in (sort(number), sort(upos), sort(ipos), bounds, places):
        out = out + jnp.pad(piece, (at, LISTS - at - piece.shape[0]))
        at += piece.shape[0]
    return out


def body(tiles, tile_user, tile_item, row_lengths, start_panel):
    tiles = tiles.reshape(NT, TB, TB)
    user_block = tile_user.reshape(NT)
    item_block = tile_item.reshape(NT)
    part, stacked, where = first_product(
        user_block, item_block, tiles, row_lengths.reshape(NT, TB), start_panel.T
    )
    upos = place_of(user_block, where[0, :NT])
    ipos = item_places(item_block, where[1, :NT])
    places = place_of(jnp.arange(UB, dtype=jnp.int32), where[0, :UB])
    lists = tile_lists(upos, ipos, places)
    halves = (0, 0), (0, 1), (3, 0), (3, 1), (1, 0), (1, 1), (2, 0), (2, 1)
    quarters, odd = (jnp.array(column, jnp.int32) for column in zip(*halves))
    base = ((where[1, :8] + quarters) % 4) * (QB * TB) + odd * (HB * TB)
    users = sum_over_item(part)
    terms = scatter(users, lists, stacked)
    own_a, own_b = (terms[0] + terms[1]) + terms[2], (terms[3] + terms[4]) + terms[5]
    down_a, up_b = user_move(own_a, 1), user_move(own_b, -1)
    down_b, up_a = user_move(own_b, 1), user_move(own_a, -1)
    far = user_move(down_a, 1), user_move(up_b, -1)
    before = forth_product(3, 4, OWN_A, lists, stacked, (own_a, own_b))
    before = forth_product(1, 3, UP_B, lists, stacked, (up_b, down_a, up_a, down_b), before)
    (part,) = forth_product(0, 1, FAR_A, lists, stacked, far, before, True)
    users = sum_over_item(part)
    terms = scatter(users, lists, stacked)
    own = scale_sum(inverse_beside(lists, users), terms)
    down, up = user_move(own, 1), user_move(own, -1)
    gram = sum_all_user(sum_all_item(gram_product(own)))
    gram, down, up = lax.optimization_barrier((gram, down, up))
    far = user_move(down[:HB], 1), user_move(up[HB:], -1)
    inverse = inverse_lower(gram)
    cuts = (0, 0), (0, HB), (1, 0), (1, HB), (2, 0), (2, HB)
    panel = final_product(base[:6], inverse, (own, down, up), cuts)
    return final_product(base[6:], inverse, far, ((0, 0), (1, 0)), panel).T


def solution(mesh):
    placed = (
        P("user", "item", None, None),
        P("user", "item"),
        P("user", "item"),
        P("user", "item", None),
        P("item", None),
    )
    return jax.shard_map(
        body, mesh=mesh, in_specs=placed, out_specs=P("item", None), check_vma=False
    )
```

```python
import functools

import jax
import jax.numpy as jnp
from jax import lax
from jax.experimental import pallas as pl
from jax.experimental.pallas import tpu as pltpu
from jax.sharding import PartitionSpec as P

ITERS = 2
TB = 128
K = 64
NT = 192
IB = 128
UB = 32
QB = 32
HB = 16
ITEMS = 524288
GROUP = 48
RUN = 32
VMEM = pl.BlockSpec(memory_space=pltpu.VMEM)
SMEM = pl.BlockSpec(memory_space=pltpu.SMEM)
ANY = pl.BlockSpec(memory_space=pl.ANY)
MIB = 1024 * 1024
F32, BF16 = jnp.float32, jnp.bfloat16


def cost(us):
    return pl.CostEstimate(flops=0, bytes_accessed=int(us * 3.5e6), transcendentals=0)


def split2(x):
    hi = x.astype(BF16)
    lo = (x - hi.astype(F32)).astype(BF16)
    return hi, lo


def split3(x):
    hi = x.astype(BF16)
    rest = x - hi.astype(F32)
    mid = rest.astype(BF16)
    lo = (rest - mid.astype(F32)).astype(BF16)
    return hi, mid, lo


def times_nt(block, stacked):
    left = jnp.concatenate(split2(block), axis=0)
    full = lax.dot_general(left, stacked, (((1,), (1,)), ((), ())), preferred_element_type=F32)
    half = full[:K] + full[K:]
    return half[:, :TB] + half[:, TB:]


def times_nn(block, stacked):
    hi, lo = split2(block)
    left = jnp.concatenate(
        [jnp.concatenate([hi, hi], axis=1), jnp.concatenate([lo, lo], axis=1)], axis=0
    )
    full = lax.dot_general(left, stacked, (((1,), (0,)), ((), ())), preferred_element_type=F32)
    return full[:K] + full[K:]


def place_of(user_block, spot):
    core = (user_block >> 4) ^ (spot & 1)
    x = ((user_block >> 2) - (spot >> 1)) & 3
    y = (user_block - (spot >> 3)) & 3
    return core * 16 + x * 4 + y


def first_kernel(tiles, panel, user_in, item_in, lengths_in, users, stacked, where, user, item, lengths, sems):
    step = pl.program_id(0)
    spot = lax.axis_index("item")

    @pl.when(step == 0)
    def _():
        pairs = (lengths_in, lengths), (user_in, user), (item_in, item)
        copies = [
            pltpu.make_async_copy(source, target, sems.at[number])
            for number, (source, target) in enumerate(pairs)
        ]
        for copy in copies:
            copy.start()
        users[...] = jnp.zeros_like(users)
        rows = lax.broadcasted_iota(jnp.int32, where.shape, 0)
        where[...] = jnp.where(rows == 0, spot, lax.axis_index("user"))
        for copy in copies:
            copy.wait()

    columns = lax.broadcasted_iota(jnp.int32, (TB, TB), 1)
    ends = lengths[pl.ds(pl.multiple_of(step * GROUP, GROUP), GROUP)].T
    parts = []
    for t in range(GROUP):
        n = step * GROUP + t
        masked = jnp.where(columns < ends[:, t : t + 1], tiles[t], 0.0)
        both = jnp.concatenate(split2(masked), axis=0)
        stacked[t] = both
        block = panel[:, pl.ds(pl.multiple_of(item[n] * TB, TB), TB)]
        parts.append((place_of(user[n], spot), times_nt(block, both)))
    for at, value in parts:
        users[at] += value


def first_product(user, item, tiles, lengths, panel_t):
    return pl.pallas_call(
        first_kernel,
        out_shape=(
            jax.ShapeDtypeStruct((UB, K, TB), F32),
            jax.ShapeDtypeStruct((NT, 2 * TB, TB), BF16),
            jax.ShapeDtypeStruct((8, 2 * TB), jnp.int32),
        ),
        grid=(NT // GROUP,),
        in_specs=[
            pl.BlockSpec((GROUP, TB, TB), lambda s: (s, 0, 0)),
            pl.BlockSpec((K, IB * TB), lambda s: (0, 0)),
        ]
        + [pl.BlockSpec(memory_space=pltpu.HBM)] * 3,
        out_specs=[
            pl.BlockSpec((UB, K, TB), lambda s: (0, 0, 0)),
            pl.BlockSpec((GROUP, 2 * TB, TB), lambda s: (s, 0, 0)),
            pl.BlockSpec((8, 2 * TB), lambda s: (0, 0)),
        ],
        scratch_shapes=[
            pltpu.SMEM((NT,), jnp.int32),
            pltpu.SMEM((NT,), jnp.int32),
            pltpu.VMEM((NT, TB), jnp.int32),
            pltpu.SemaphoreType.DMA((3,)),
        ],
        cost_estimate=cost(10.0),
        compiler_params=pltpu.CompilerParams(vmem_limit_bytes=28 * MIB),
    )(*(pltpu.with_memory_space_constraint(x, pltpu.HBM) for x in (tiles, panel_t, user, item, lengths)))


def each_tile(first, last, lists, stacked, total, use):
    start, end = lists[3 * NT + first], lists[3 * NT + last]

    def step(g, carry):
        parts = []
        for t in range(RUN):
            j = start + g * RUN + t
            at = jnp.minimum(j, end - 1)
            spot, value = use(lists[NT + at], lists[2 * NT + at], stacked[lists[at]])
            parts.append((spot, jnp.where(j < end, value, 0.0)))
        for spot, value in parts:
            total[spot, :K] += value
        return carry

    lax.fori_loop(0, (end - start + RUN - 1) >> 5, step, 0)


def back_kernel(first, last, shift, sizes, lists, users, stacked, *rest):
    outs = rest[: len(sizes)]
    (total,) = rest[len(sizes) :]
    total[...] = jnp.zeros_like(total)

    def use(user, item, tile):
        return item - shift * HB, times_nn(users[user, :K], tile)

    each_tile(first, last, lists, stacked, total, use)
    at = 0
    for size, out in zip(sizes, outs):
        out[...] = total[at : at + size]
        at += size


def back_product(first, last, shift, sizes, lists, users, stacked):
    return pl.pallas_call(
        functools.partial(back_kernel, first, last, shift, sizes),
        out_shape=[jax.ShapeDtypeStruct((size, K, TB), F32) for size in sizes],
        in_specs=[SMEM, VMEM, VMEM],
        out_specs=[VMEM] * len(sizes),
        scratch_shapes=[pltpu.VMEM((sum(sizes), K, TB), F32)],
        cost_estimate=cost(2.5 + 0.04 * sum(sizes)),
        compiler_params=pltpu.CompilerParams(vmem_limit_bytes=8 * MIB),
    )(lists, users, stacked)


def gram_of(blocks):
    total = jnp.zeros((3 * K, 3 * K), F32)
    for first, second in zip(blocks[::2], blocks[1::2]):
        three = jnp.concatenate(split3(jnp.concatenate([first, second], axis=1)), axis=0)
        total += lax.dot_general(three, three, (((1,), (1,)), ((), ())), preferred_element_type=F32)
    rows = (total[2 * K :] + total[K : 2 * K]) + total[:K]
    return (rows[:, 2 * K :] + rows[:, K : 2 * K]) + rows[:, :K]


def forth_kernel(first, last, shift, count, more, final, lists, stacked, *rest):
    ins = rest[:count]
    rest = rest[count:]
    if more:
        before, gram_before, rest = rest[0], rest[1], rest[2:]
    if final:
        out, panel = rest
        out[...] = jnp.zeros_like(out)
    else:
        out, gram, panel = rest
    out[:, :K] = before[...] if more else jnp.zeros((UB, K, TB), F32)
    for place, piece in enumerate(ins):
        panel[place * HB : (place + 1) * HB] = piece[...]

    def use(user, item, tile):
        return user, times_nt(panel[item - shift * HB], tile)

    own = gram_of([panel[b] for b in range(count * HB)])
    if more:
        own = own + gram_before[...]
    if final:
        for b in range(UB):
            out[lists[PLACE_AT + b], K : K + 2, :K] = own[2 * b : 2 * b + 2]
    else:
        gram[...] = own
    each_tile(first, last, lists, stacked, out, use)


def forth_product(first, last, shift, lists, stacked, pieces, before=None, final=False):
    more = before is not None
    args = list(pieces) + (list(before) if more else [])
    shapes = [jax.ShapeDtypeStruct((UB, K, TB), F32), jax.ShapeDtypeStruct((K, K), F32)]
    if final:
        shapes = [jax.ShapeDtypeStruct((UB, K + 8, TB), F32)]
    return pl.pallas_call(
        functools.partial(forth_kernel, first, last, shift, len(pieces), more, final),
        out_shape=shapes,
        in_specs=[SMEM] + [VMEM] * (1 + len(args)),
        out_specs=[VMEM] * len(shapes),
        scratch_shapes=[pltpu.VMEM((len(pieces) * HB, K, TB), F32)],
        cost_estimate=cost(3.0 + 0.8 * len(pieces)),
        compiler_params=pltpu.CompilerParams(vmem_limit_bytes=8 * MIB),
    )(lists, stacked, *args)


def gram_kernel(own, out):
    out[...] = gram_of([own[b] for b in range(QB)])


def gram_product(own):
    return pl.pallas_call(
        gram_kernel,
        out_shape=jax.ShapeDtypeStruct((K, K), F32),
        in_specs=[VMEM],
        out_specs=VMEM,
        cost_estimate=cost(0.7),
        compiler_params=pltpu.CompilerParams(vmem_limit_bytes=4 * MIB),
    )(own)


def inverse_of(gram):
    rows = lax.broadcasted_iota(jnp.int32, (K, 2 * K), 0)
    lanes = lax.broadcasted_iota(jnp.int32, (K, 2 * K), 1)
    unit = (lanes == rows + K).astype(F32)
    left = gram * F32(1.0 / ITEMS)
    work = jnp.concatenate([left, jnp.zeros((K, K), F32)], axis=1) + unit
    for k in range(K):
        pivot = work[k : k + 1, k : k + 1]
        scaled = work[k : k + 1, :] * lax.rsqrt(pivot)
        column = work[:, k : k + 1] * lax.rsqrt(pivot)
        lower = work - column * scaled
        work = jnp.where(rows > k, lower, jnp.where(rows == k, scaled, work))
    return work[:, K:]


def inverse_kernel(gram, out):
    out[...] = inverse_of(gram[...])


def inverse_lower(gram):
    return pl.pallas_call(
        inverse_kernel,
        out_shape=jax.ShapeDtypeStruct((K, K), F32),
        in_specs=[VMEM],
        out_specs=VMEM,
        cost_estimate=cost(6.7),
        compiler_params=pltpu.CompilerParams(vmem_limit_bytes=2 * MIB),
    )(gram)


def inverse_beside_kernel(lists, users, out, gram):
    for b in range(UB):
        gram[2 * b : 2 * b + 2] = users[lists[PLACE_AT + b], K : K + 2, :K]
    out[...] = inverse_of(gram[...])


def inverse_beside(lists, users):
    return pl.pallas_call(
        inverse_beside_kernel,
        out_shape=jax.ShapeDtypeStruct((K, K), F32),
        in_specs=[SMEM, VMEM],
        out_specs=VMEM,
        scratch_shapes=[pltpu.VMEM((K, K), F32)],
        cost_estimate=cost(6.9),
        compiler_params=pltpu.CompilerParams(vmem_limit_bytes=2 * MIB),
    )(lists, users)


def exact_left(inverse):
    high, mid, low = split3(inverse)
    return jnp.concatenate([high, high, mid, mid], axis=1), jnp.concatenate([high, low], axis=1)


def exact_times(left, block):
    high, mid, low = split3(block)
    large = jnp.concatenate([high, mid, high, mid], axis=0)
    small = jnp.concatenate([low, high], axis=0)
    return jnp.dot(left[1], small, preferred_element_type=F32) + jnp.dot(
        left[0], large, preferred_element_type=F32
    )


def scale_kernel(inverse, *refs):
    left = exact_left(inverse[...])
    out = refs[-1]
    for half in range(2):
        first, second, third = refs[3 * half : 3 * half + 3]
        for b in range(HB):
            out[half * HB + b] = exact_times(left, (first[b] + second[b]) + third[b])


def scale_sum(inverse, terms):
    return pl.pallas_call(
        scale_kernel,
        out_shape=jax.ShapeDtypeStruct((QB, K, TB), F32),
        in_specs=[VMEM] * 7,
        out_specs=VMEM,
        cost_estimate=cost(0.9),
        compiler_params=pltpu.CompilerParams(vmem_limit_bytes=4 * MIB),
    )(inverse, *terms)


def final_kernel(cuts, base, inverse, *refs):
    out, made, sems = refs[-3:]
    left = exact_left(inverse[...])
    copies = []
    for place, (number, start) in enumerate(cuts):
        for b in range(HB):
            made[place, :, b * TB : (b + 1) * TB] = exact_times(left, refs[number][start + b])
        at = pl.multiple_of(base[place], HB * TB)
        copy = pltpu.make_async_copy(
            made.at[place], out.at[:, pl.ds(at, HB * TB)], sems.at[place]
        )
        copy.start()
        copies.append(copy)
    for copy in copies:
        copy.wait()


def final_product(base, inverse, arrays, cuts, before=None):
    more = [] if before is None else [before]
    return pl.pallas_call(
        functools.partial(final_kernel, cuts),
        out_shape=jax.ShapeDtypeStruct((K, IB * TB), F32),
        in_specs=[SMEM] + [VMEM] * (1 + len(arrays)) + [ANY] * len(more),
        out_specs=ANY,
        scratch_shapes=[
            pltpu.VMEM((len(cuts), K, HB * TB), F32),
            pltpu.SemaphoreType.DMA((len(cuts),)),
        ],
        input_output_aliases={2 + len(arrays): 0} if more else {},
        cost_estimate=cost(1.0 + 0.5 * len(cuts)),
        compiler_params=pltpu.CompilerParams(vmem_limit_bytes=8 * MIB),
    )(base, inverse, *arrays, *more)


def user_move(value, by):
    return lax.ppermute(value, "user", [(s, (s + by) % 4) for s in range(4)])


def item_move(value, dy=0, dx=0, dc=0):
    pairs = []
    for y in range(4):
        for x in range(4):
            for c in range(2):
                to = (((y + dy) % 4) * 4 + (x + dx) % 4) * 2 + (c + dc) % 2
                pairs.append(((y * 4 + x) * 2 + c, to))
    return lax.ppermute(value, "item", pairs)


def sum_over_item(part):
    mine = part[:16] + item_move(part[16:], dc=1)
    near, right, far, left = mine[:4], mine[4:8], mine[8:12], mine[12:]
    mine = near + item_move(right, dx=1) + item_move(left, dx=-1) + item_move(far, dx=2)
    one, two, three = item_move(mine, dy=1), item_move(mine, dy=2), item_move(mine, dy=-1)
    mine = (mine + jnp.roll(two, 2, 0)) + (jnp.roll(one, -1, 0) + jnp.roll(three, 1, 0))
    left, far, right = item_move(mine, dx=1), item_move(mine, dx=2), item_move(mine, dx=-1)
    mine = jnp.concatenate([mine, right, far, left], axis=0)
    return jnp.concatenate([mine, item_move(mine, dc=1)], axis=0)


def sum_all_user(value):
    return (value + user_move(value, 2)) + (user_move(value, 1) + user_move(value, -1))


def sum_all_item(value):
    value = value + item_move(value, dc=1)
    value = (value + item_move(value, dx=2)) + (item_move(value, dx=1) + item_move(value, dx=-1))
    return (value + item_move(value, dy=2)) + (item_move(value, dy=1) + item_move(value, dy=-1))


FAR_A, FAR_B, UP_B, DOWN_A, UP_A, DOWN_B, OWN_A, OWN_B = range(8)
PLACES = {0: (OWN_A, OWN_B), 1: (UP_A, UP_B), 2: (FAR_A, FAR_B), 3: (DOWN_A, DOWN_B)}
BOUNDS = (0, UP_B, UP_A, OWN_A, 8)
PLACE_AT = 3 * NT + len(BOUNDS)
LISTS = 640


def scatter(users, lists, stacked):
    far_a, far_b = back_product(0, 1, FAR_A, (HB, HB), lists, users, stacked)
    got_a, got_b = user_move(far_a, 1), user_move(far_b, -1)
    up_b, down_a = back_product(1, 2, UP_B, (HB, HB), lists, users, stacked)
    direct_b, direct_a = user_move(up_b, 1), user_move(down_a, -1)
    up_a, down_b, own_a, own_b = back_product(2, 4, UP_A, (HB,) * 4, lists, users, stacked)
    sum_a, sum_b = user_move(up_a + got_a, 1), user_move(down_b + got_b, -1)
    return lax.optimization_barrier((own_a, direct_a, sum_a, own_b, direct_b, sum_b))


def item_places(item_block, z):
    quarter = (item_block // QB - z) % 4
    half = (item_block // HB) % 2
    place = jnp.zeros_like(quarter)
    for at, (first, second) in PLACES.items():
        place = jnp.where(quarter == at, jnp.where(half == 0, first, second), place)
    return place * HB + item_block % HB


def tile_lists(upos, ipos, places):
    number = jnp.arange(NT, dtype=jnp.int32)
    key = ipos * NT + number
    rank = jnp.sum((key[None, :] < key[:, None]).astype(jnp.int32), axis=1)
    spot = rank[None, :] == number[:, None]

    def sort(values):
        return jnp.sum(jnp.where(spot, values[None, :], 0), axis=1)

    ends = jnp.array(BOUNDS, jnp.int32) * HB
    bounds = jnp.sum((ipos[None, :] < ends[:, None]).astype(jnp.int32), axis=1)
    out = jnp.zeros((LISTS,), jnp.int32)
    at = 0
    for piece in (sort(number), sort(upos), sort(ipos), bounds, places):
        out = out + jnp.pad(piece, (at, LISTS - at - piece.shape[0]))
        at += piece.shape[0]
    return out


def body(tiles, tile_user, tile_item, row_lengths, start_panel):
    tiles = tiles.reshape(NT, TB, TB)
    user_block = tile_user.reshape(NT)
    item_block = tile_item.reshape(NT)
    part, stacked, where = first_product(
        user_block, item_block, tiles, row_lengths.reshape(NT, TB), start_panel.T
    )
    upos = place_of(user_block, where[0, :NT])
    ipos = item_places(item_block, where[1, :NT])
    places = place_of(jnp.arange(UB, dtype=jnp.int32), where[0, :UB])
    lists = tile_lists(upos, ipos, places)
    halves = (0, 0), (0, 1), (3, 0), (3, 1), (1, 0), (1, 1), (2, 0), (2, 1)
    quarters, odd = (jnp.array(column, jnp.int32) for column in zip(*halves))
    base = ((where[1, :8] + quarters) % 4) * (QB * TB) + odd * (HB * TB)
    users = sum_over_item(part)
    terms = scatter(users, lists, stacked)
    own_a, own_b = (terms[0] + terms[1]) + terms[2], (terms[3] + terms[4]) + terms[5]
    down_a, up_b = user_move(own_a, 1), user_move(own_b, -1)
    down_b, up_a = user_move(own_b, 1), user_move(own_a, -1)
    far = user_move(down_a, 1), user_move(up_b, -1)
    before = forth_product(3, 4, OWN_A, lists, stacked, (own_a, own_b))
    before = forth_product(1, 3, UP_B, lists, stacked, (up_b, down_a, up_a, down_b), before)
    (part,) = forth_product(0, 1, FAR_A, lists, stacked, far, before, True)
    users = sum_over_item(part)
    terms = scatter(users, lists, stacked)
    own = scale_sum(inverse_beside(lists, users), terms)
    down, up = user_move(own, 1), user_move(own, -1)
    gram = sum_all_user(sum_all_item(gram_product(own)))
    gram, down, up = lax.optimization_barrier((gram, down, up))
    far = user_move(down[:HB], 1), user_move(up[HB:], -1)
    inverse = inverse_lower(gram)
    cuts = (0, 0), (0, HB), (1, 0), (1, HB), (2, 0), (2, HB)
    panel = final_product(base[:6], inverse, (own, down, up), cuts)
    return final_product(base[6:], inverse, far, ((0, 0), (1, 0)), panel).T


def solution(mesh):
    placed = (
        P("user", "item", None, None),
        P("user", "item"),
        P("user", "item"),
        P("user", "item", None),
        P("item", None),
    )
    return jax.shard_map(
        body, mesh=mesh, in_specs=placed, out_specs=P("item", None), check_vma=False
    )
```
